32 devices in a mesh: seq: 8 (over z, x), fsdp: 4 (over y, core).
Axes of the slice: x: 2, y: 2, z: 4, core: 2. Of those that a mesh axis runs over, the one named last changes fastest.
Arguments:
- image_query: bfloat16 [4, 2048, 1536], P('fsdp', 'seq'), may hold values from -6 to 6
- image_key: bfloat16 [4, 2048, 1536], P('fsdp', 'seq'), may hold values from -6 to 6
- image_value: bfloat16 [4, 2048, 1536], P('fsdp', 'seq'), may hold values from -6 to 6
- text_key: bfloat16 [4, 512, 1536], P('fsdp'), may hold values from -6 to 6
- text_value: bfloat16 [4, 512, 1536], P('fsdp'), may hold values from -6 to 6
- out_weight: bfloat16 [1536, 1536], P('fsdp'), may hold values from -0.15625 to 0.15625
- cotangent: bfloat16 [4, 2048, 1536], P('fsdp', 'seq'), may hold values from -6 to 6
Outputs:
- image_out: bfloat16 [4, 2048, 1536], P('fsdp', 'seq')
- grad_query: bfloat16 [4, 2048, 1536], P('fsdp', 'seq')
- grad_key: bfloat16 [4, 2048, 1536], P('fsdp', 'seq')
- grad_value: bfloat16 [4, 2048, 1536], P('fsdp', 'seq')
- grad_weight: float32 [1536, 1536], P(('fsdp', 'seq'))
The draws below stay inside these ranges and needn't reach their ends.
All inputs are finite; a program needn't handle non-finite values.
Results may differ from the reference program's by a relative error of at most 0.0095.
Values may be sent and summed in bfloat16 or wider, within the bound.
No kernel may reach another device: no remote copies, remote signals or barrier semaphores. Data moves between devices by JAX's collectives and lax.ppermute only.
A program may use at most 128 MiB of HBM per device.

```python
import math
import jax
import jax.numpy as jnp
from jax import lax

HEAD_DIM = 128
OUT_WIDTH = 1536
TEXT = 512
STEPS = 4
TOK_DEV = 256
INNER = 1536
IMAGE = 2048
SAMPLES = 4
N_SEQ = 8


def draw_image_query(key, part):
    shape = (SAMPLES, IMAGE, INNER)
    base = jnp.clip(jax.random.normal(jax.random.fold_in(key, 11), shape, jnp.float32), -5.0, 5.0)
    return base.astype(jnp.bfloat16)


def draw_image_key(key, part):
    shape = (SAMPLES, IMAGE, INNER)
    base = jnp.clip(jax.random.normal(jax.random.fold_in(key, 21), shape, jnp.float32), -5.0, 5.0)
    return base.astype(jnp.bfloat16)


def spiked(entries, key, source, target, parts, factor):
    def block_of(axis_at):
        return (jnp.arange(entries.shape[axis_at]) // (entries.shape[axis_at] // parts)).reshape((-1,) + (1,) * (entries.ndim - 1 - axis_at))

    first = jax.random.permutation(key, parts)[block_of(target)]
    far = (block_of(target) + parts // 2) % parts
    return jnp.where((block_of(source) == first) | (block_of(source) == far), factor * entries, entries)


def shard_levels(rng, shape, pieces, smallest, high):
    def one(dim, parts):
        steps = jax.random.uniform(jax.random.fold_in(jax.random.fold_in(rng, 6), dim), (parts,), jnp.float32, smallest / len(pieces), high / len(pieces))
        return jnp.repeat(jnp.exp(steps), shape[dim] // parts).reshape((-1,) + (1,) * (len(shape) - dim - 1))

    gain = one(*pieces[0])
    for cut in pieces[1:]:
        gain = gain * one(*cut)
    return gain


def centred(stream_key, dims, spread, reach, cuts=(), held_as=jnp.bfloat16):
    gain = shard_levels(stream_key, dims, cuts, -0.22, 0.18) if cuts else 1.0
    entries = jax.random.normal(stream_key, dims, jnp.float32) * spread * gain
    return jnp.minimum(jnp.maximum(entries, -reach), reach).astype(held_as)


def gaussian_with(key, extent, spread, bound, pieces, heavy, held_as=jnp.bfloat16):
    drawn = spread * jax.random.normal(key, extent, jnp.float32)
    if pieces:
        drawn = drawn * shard_levels(key, extent, pieces, -0.22, 0.18)
    return jnp.clip(spiked(drawn, jax.random.fold_in(key, 3), *heavy), -bound, bound).astype(held_as)


def setup_inputs(seed: int = 0) -> dict:
    streams_of = jax.random.split(jax.random.key(seed), 8)
    return {
        "image_query": draw_image_query(jax.random.fold_in(streams_of[7], 71), 0),
        "image_key": draw_image_key(jax.random.fold_in(streams_of[7], 71), 0),
        "image_value": centred(streams_of[2], (SAMPLES, IMAGE, INNER), 1.0, 6.0, ((0, 4), (1, 8))),
        "text_key": centred(streams_of[3], (SAMPLES, TEXT, INNER), 1.0, 6.0, ((0, 4),)),
        "text_value": centred(streams_of[4], (SAMPLES, TEXT, INNER), 1.0, 6.0, ((0, 4),)),
        "out_weight": centred(streams_of[5], (INNER, OUT_WIDTH), INNER ** -0.5, 0.15625, ((0, 4),)),
        "cotangent": gaussian_with(streams_of[6], (SAMPLES, IMAGE, OUT_WIDTH), 1.0, 6.0, ((0, 4), (1, 8)), (1, 2, 8, 2.0)),
    }


def head_pass(inputs):
    head_query, head_key, head_value, head_grad = inputs
    scaling = 1.0 / math.sqrt(head_query.shape[1])
    scores = lax.dot_general(head_query, head_key, (((1,), (1,)), ((), ())), preferred_element_type=jnp.float32) * scaling
    row_peak = lax.optimization_barrier(jnp.max(scores, axis=1, keepdims=True))
    shifted = jnp.exp(scores - row_peak)
    softmax = shifted / lax.optimization_barrier(jnp.sum(shifted, axis=1, keepdims=True))
    prob_low = softmax.astype(jnp.bfloat16)
    attended = jnp.dot(prob_low, head_value, preferred_element_type=jnp.float32).astype(jnp.bfloat16)
    row_delta = lax.optimization_barrier(jnp.sum(head_grad.astype(jnp.float32) * attended.astype(jnp.float32), axis=1, keepdims=True))
    grad_prob = lax.dot_general(head_grad, head_value, (((1,), (1,)), ((), ())), preferred_element_type=jnp.float32)
    grad_score = (softmax * (grad_prob - row_delta) * scaling).astype(jnp.bfloat16)
    grad_q = jnp.dot(grad_score, head_key, preferred_element_type=jnp.float32).astype(jnp.bfloat16)
    grad_k = lax.dot_general(grad_score, head_query, (((0,), (0,)), ((), ())), preferred_element_type=jnp.float32)
    grad_v = lax.dot_general(prob_low, head_grad, (((0,), (0,)), ((), ())), preferred_element_type=jnp.float32)
    return (attended, grad_q, grad_k, grad_v)

def split_heads(matrix, width):
    return matrix.reshape(matrix.shape[0], -1, width).transpose(1, 0, 2)

def merge_heads(stacked):
    return stacked.transpose(1, 0, 2).reshape(stacked.shape[1], -1)

def reference(image_query, image_key, image_value, text_key, text_value, out_weight, cotangent):
    out_list, query_list, key_list, value_list = ([], [], [], [])
    grad_weight = jnp.zeros((INNER, OUT_WIDTH), jnp.float32)
    for sample in range(SAMPLES):
        queries = image_query[sample]
        keys_all = image_key[sample]
        values_all = image_value[sample]
        grad_attended = lax.dot_general(cotangent[sample], out_weight, (((1,), (1,)), ((), ())), preferred_element_type=jnp.float32).astype(jnp.bfloat16)

        def visit_block(running, block_index):
            key_sum, value_sum = running
            window = ((block_index - STEPS + 1) * TOK_DEV + jnp.arange(STEPS * TOK_DEV, dtype=jnp.int32)) % IMAGE
            window = window.astype(jnp.int32)
            first_row = (block_index * TOK_DEV).astype(jnp.int32)
            block_query = lax.dynamic_slice_in_dim(queries, first_row, TOK_DEV, 0)
            block_grad = lax.dynamic_slice_in_dim(grad_attended, first_row, TOK_DEV, 0)
            set_keys = jnp.concatenate([text_key[sample], jnp.take(keys_all, window, axis=0)], axis=0)
            set_values = jnp.concatenate([text_value[sample], jnp.take(values_all, window, axis=0)], axis=0)
            attended, grad_q, grad_k, grad_v = lax.map(head_pass, (split_heads(block_query, HEAD_DIM), split_heads(set_keys, HEAD_DIM), split_heads(set_values, HEAD_DIM), split_heads(block_grad, HEAD_DIM)))
            key_sum = key_sum.at[window].add(merge_heads(grad_k)[TEXT:])
            value_sum = value_sum.at[window].add(merge_heads(grad_v)[TEXT:])
            return ((key_sum, value_sum), (merge_heads(attended), merge_heads(grad_q)))
        empty_sum = jnp.zeros((IMAGE, INNER), jnp.float32)
        (key_sum, value_sum), (attended, grad_q) = lax.scan(visit_block, (empty_sum, empty_sum), jnp.arange(N_SEQ, dtype=jnp.int32))
        attended = attended.reshape(IMAGE, INNER)
        grad_q = grad_q.reshape(IMAGE, INNER)
        out_list.append(jnp.dot(attended, out_weight, preferred_element_type=jnp.float32).astype(jnp.bfloat16))
        grad_weight = grad_weight + lax.dot_general(attended, cotangent[sample], (((0,), (0,)), ((), ())), preferred_element_type=jnp.float32)
        query_list.append(grad_q)
        key_list.append(key_sum.astype(jnp.bfloat16))
        value_list.append(value_sum.astype(jnp.bfloat16))
    return (jnp.stack(out_list), jnp.stack(query_list), jnp.stack(key_list), jnp.stack(value_list), grad_weight)
```

```python
import functools
import math

import jax
import jax.numpy as jnp
from jax import lax
from jax.experimental import pallas as pl
from jax.experimental.pallas import tpu as pltpu
from jax.sharding import PartitionSpec as P

HEAD_DIM = 128
STEPS = 4
F32 = jnp.float32
BF16 = jnp.bfloat16


def rows_dot(a, b):
    return lax.dot_general(a, b, (((1,), (1,)), ((), ())), preferred_element_type=F32)


def cols_dot(a, b):
    return lax.dot_general(a, b, (((0,), (0,)), ((), ())), preferred_element_type=F32)


def attention_body(
    place, q_own, q_par, k_own, v_own, kv_par, near_own, near_par, far, t_k, t_v, g_own, g_par,
    od_own, od_par, d_own, d_par, d_near_own, d_near_par, d_far,
    k_all, v_all, dk_all, dv_all,
):
    tokens = q_own.shape[0]
    col = place[1]
    scale = 1.0 / math.sqrt(q_own.shape[1])
    to_log2 = scale * math.log2(math.e)

    def block(first, which):
        return pl.ds(pl.multiple_of((first + which) * tokens, tokens), tokens)

    at_far = pl.ds(0, tokens)
    at_near_own, at_near_par = block(1, col), block(1, 1 - col)
    at_own, at_par = block(3, col), block(3, 1 - col)
    k_all[at_far] = far[0]
    v_all[at_far] = far[1]
    k_all[at_near_own] = near_own[0]
    v_all[at_near_own] = near_own[1]
    k_all[at_near_par] = near_par[0]
    v_all[at_near_par] = near_par[1]
    k_all[at_own] = k_own[...]
    v_all[at_own] = v_own[...]
    k_all[at_par] = kv_par[0]
    v_all[at_par] = kv_par[1]
    dk_all[...] = jnp.zeros_like(dk_all)
    dv_all[...] = jnp.zeros_like(dv_all)

    def one(q_ref, g_ref, od_ref, first):
        window = pl.ds(pl.multiple_of(first * tokens, tokens), STEPS * tokens)
        q = q_ref[...]
        g = g_ref[...]
        s_t = rows_dot(q, t_k[...])
        s_i = rows_dot(q, k_all[window])
        peak = jnp.maximum(jnp.max(s_t, axis=1, keepdims=True), jnp.max(s_i, axis=1, keepdims=True))
        e_t = jnp.exp2((s_t - peak) * to_log2)
        e_i = jnp.exp2((s_i - peak) * to_log2)
        total = jnp.sum(e_t, axis=1, keepdims=True) + jnp.sum(e_i, axis=1, keepdims=True)
        inverse = 1.0 / total
        p_t = e_t * inverse
        p_i = e_i * inverse
        low_t = p_t.astype(BF16)
        low_i = p_i.astype(BF16)
        out = jnp.dot(low_t, t_v[...], preferred_element_type=F32)
        out += jnp.dot(low_i, v_all[window], preferred_element_type=F32)
        out = out.astype(BF16)
        od_ref[0] = out
        delta = jnp.sum(g.astype(F32) * out.astype(F32), axis=1, keepdims=True)
        ds_t = (p_t * ((rows_dot(g, t_v[...]) - delta) * scale)).astype(BF16)
        ds_i = (p_i * ((rows_dot(g, v_all[window]) - delta) * scale)).astype(BF16)
        dq = jnp.dot(ds_t, t_k[...], preferred_element_type=F32)
        dq += jnp.dot(ds_i, k_all[window], preferred_element_type=F32)
        od_ref[1] = dq.astype(BF16)
        dk_all[window] += cols_dot(ds_i, q)
        dv_all[window] += cols_dot(low_i, g)

    one(q_own, g_own, od_own, col)
    one(q_par, g_par, od_par, 1 - col)
    for ref, rows in (
        (d_own, at_own), (d_par, at_par), (d_near_own, at_near_own), (d_near_par, at_near_par), (d_far, at_far),
    ):
        ref[0] = dk_all[rows].astype(BF16)
        ref[1] = dv_all[rows].astype(BF16)


def attention(place, q, q_par, k, v, kv_par, near_own, near_par, far, t_k, t_v, g_own, g_par):
    tokens = q.shape[0]
    width = q_par.shape[1]
    text = t_k.shape[0]
    heads = width // HEAD_DIM
    whole = lambda rows: pl.BlockSpec((rows, HEAD_DIM), lambda h, place: (0, place[0] * heads + h))
    part = pl.BlockSpec((tokens, HEAD_DIM), lambda h, place: (0, h))
    double = pl.BlockSpec((2, tokens, HEAD_DIM), lambda h, place: (0, 0, h))
    keys = text + STEPS * tokens
    macs = heads * 2 * tokens * HEAD_DIM * (4 * keys + 2 * STEPS * tokens)
    out = jax.ShapeDtypeStruct((2, tokens, width), BF16)
    image_rows = (STEPS + 1) * tokens
    return pl.pallas_call(
        attention_body,
        out_shape=(out,) * 7,
        grid_spec=pltpu.PrefetchScalarGridSpec(
            num_scalar_prefetch=1,
            grid=(heads,),
            in_specs=[whole(tokens), part, whole(tokens), whole(tokens), double, double, double, double,
                      whole(text), whole(text), part, part],
            out_specs=[double] * 7,
            scratch_shapes=[
                pltpu.VMEM((image_rows, HEAD_DIM), BF16),
                pltpu.VMEM((image_rows, HEAD_DIM), BF16),
                pltpu.VMEM((image_rows, HEAD_DIM), F32),
                pltpu.VMEM((image_rows, HEAD_DIM), F32),
            ],
        ),
        compiler_params=pltpu.CompilerParams(vmem_limit_bytes=48 * 1024 * 1024),
        cost_estimate=pl.CostEstimate(
            flops=4 * macs, bytes_accessed=24 * tokens * width * 2, transcendentals=heads * 2 * tokens * keys
        ),
        name="attention",
    )(place, q, q_par, k, v, kv_par, near_own, near_par, far, t_k, t_v, g_own, g_par)


def per_device(image_query, image_key, image_value, text_key, text_value, out_weight, cotangent):
    q, k, v = image_query[0], image_key[0], image_value[0]
    t_k, t_v = text_key[0], text_value[0]
    cot = cotangent[0]
    shards = lax.axis_size("fsdp")
    blocks = lax.axis_size("seq")
    pairs = blocks // 2
    groups = shards // 2
    width = out_weight.shape[0]
    tokens = q.shape[0]
    f, s = lax.axis_index("fsdp"), lax.axis_index("seq")
    col, core, row = s % 2, f % 2, f // 2

    def shift(a, axis, by):
        n = lax.axis_size(axis)
        return lax.ppermute(a, axis, [(i, (i + by) % n) for i in range(n)])

    def swap(a, axis):
        return lax.ppermute(a, axis, [(i, i ^ 1) for i in range(lax.axis_size(axis))])

    shard = [((row + 1 + g) % groups) * 2 + col for g in range(groups)]
    other = [((row + 1 + g) % groups) * 2 + 1 - col for g in range(groups)]

    def cut(a, index):
        return lax.dynamic_slice_in_dim(a, index * width, width, 1)

    def cut_two(index):
        return jnp.stack([cut(k, index), cut(v, index)])

    near_own, near_par, far, kv_par, q_par = [], [], [], [], []
    for g in range(groups):
        near_own.append(shift(cut_two(shard[g]), "seq", 2))
        kv_par.append(swap(cut_two(other[g]), "seq"))
        near_par.append(shift(kv_par[g], "seq", 2))
        far.append(shift(jnp.where(col == 0, near_par[g], near_own[g]), "seq", 2))
        q_par.append(swap(cut(q, other[g]), "seq"))
    cot_par = swap(cot, "seq")

    held = [shift(out_weight, "fsdp", -2 * (1 + g)) if g < groups - 1 else out_weight for g in range(groups)]
    weight = []
    for g in range(groups):
        from_core = swap(held[g], "fsdp")
        weight.append((jnp.where(core == col, held[g], from_core), jnp.where(core == col, from_core, held[g])))

    own_od, par_od, own_d, weight_terms = [], [], [], []
    for g in range(groups):
        g_own = rows_dot(cot, weight[g][0]).astype(BF16)
        g_par = rows_dot(cot_par, weight[g][0]).astype(BF16)
        place = jnp.stack([shard[g], col]).astype(jnp.int32)
        od_own, od_par, d_own, d_par, d_near_own, d_near_par, d_far = attention(
            place, q, q_par[g], k, v, kv_par[g], near_own[g], near_par[g], far[g], t_k, t_v, g_own, g_par
        )
        own_od.append(od_own)
        par_od.append(swap(od_par, "seq"))
        back = shift(d_far, "seq", -2).astype(F32)
        near_p = (d_near_par.astype(F32) + jnp.where(col == 0, back, 0.0)).astype(BF16)
        near_o = (d_near_own.astype(F32) + jnp.where(col == 1, back, 0.0)).astype(BF16)
        sum_p = (d_par.astype(F32) + shift(near_p, "seq", -2).astype(F32)).astype(BF16)
        from_par = swap(sum_p, "seq")
        sum_o = (d_own.astype(F32) + shift(near_o, "seq", -2).astype(F32)).astype(BF16)
        own_d.append((sum_o, from_par))
        weight_terms.append(cols_dot(od_own[0], cot) + cols_dot(od_par[0], cot_par))

    rel_out = jnp.concatenate([p for g in range(groups) for p in (own_od[g][0], par_od[g][0])], axis=1)
    rel_weight = jnp.concatenate([p for g in range(groups) for p in weight[g]], axis=0)
    image_out = jnp.dot(rel_out, rel_weight, preferred_element_type=F32).astype(BF16)

    total = None
    rows = width // blocks
    for g in range(groups):
        terms = weight_terms[g].reshape(pairs, 2, rows, -1)
        keep = lax.dynamic_index_in_dim(terms, core, 1, keepdims=False)
        give = lax.dynamic_index_in_dim(terms, 1 - core, 1, keepdims=False).astype(BF16)
        both = keep + swap(give, "fsdp").astype(F32)
        if g < groups - 1:
            both = shift(both.astype(BF16), "fsdp", 2 * (1 + g)).astype(F32)
        total = both if total is None else total + both
    z = s // 2
    mine = lax.dynamic_index_in_dim(total, z, 0, keepdims=False)
    total = total.astype(BF16)
    for by in range(1, pairs):
        there = lax.dynamic_index_in_dim(total, (z + by) % pairs, 0, keepdims=False)
        mine = mine + shift(there, "seq", 2 * by).astype(F32)
    n = blocks * shards

    def mirror(i):
        ss, ff = divmod(i, shards)
        return (ss - ss % 2 + ff % 2) * shards + ff - ff % 2 + ss % 2

    crossed = lax.ppermute(mine.astype(BF16), ("seq", "fsdp"), [(i, mirror(i)) for i in range(n)])
    grad_weight = jnp.where(core == col, mine, crossed.astype(F32))

    def assemble(pieces):
        whole = jnp.zeros((tokens, width * shards), BF16)
        for g in range(groups):
            whole = lax.dynamic_update_slice_in_dim(whole, pieces[g][0], shard[g] * width, 1)
            whole = lax.dynamic_update_slice_in_dim(whole, pieces[g][1], other[g] * width, 1)
        return whole

    grad_q = assemble([(own_od[g][1], par_od[g][1]) for g in range(groups)])
    grad_k = assemble([(own_d[g][0][0], own_d[g][1][0]) for g in range(groups)])
    grad_v = assemble([(own_d[g][0][1], own_d[g][1][1]) for g in range(groups)])
    return image_out[None], grad_q[None], grad_k[None], grad_v[None], grad_weight


def solution(mesh):
    in_specs = (
        P("fsdp", "seq", None),
        P("fsdp", "seq", None),
        P("fsdp", "seq", None),
        P("fsdp", None, None),
        P("fsdp", None, None),
        P("fsdp", None),
        P("fsdp", "seq", None),
    )
    out_specs = (
        P("fsdp", "seq", None),
        P("fsdp", "seq", None),
        P("fsdp", "seq", None),
        P("fsdp", "seq", None),
        P(("fsdp", "seq"), None),
    )
    return jax.shard_map(
        per_device, mesh=mesh, in_specs=in_specs, out_specs=out_specs, check_vma=False
    )
```

```python
import functools
import math

import jax
import jax.numpy as jnp
from jax import lax
from jax.experimental import pallas as pl
from jax.experimental.pallas import tpu as pltpu
from jax.sharding import PartitionSpec as P

HEAD_DIM = 128
STEPS = 4
F32 = jnp.float32
BF16 = jnp.bfloat16


def rows_dot(a, b):
    return lax.dot_general(a, b, (((1,), (1,)), ((), ())), preferred_element_type=F32)


def cols_dot(a, b):
    return lax.dot_general(a, b, (((0,), (0,)), ((), ())), preferred_element_type=F32)


def attention_body(
    place, q_own, q_par, k_own, v_own, kv_par, near_own, near_par, far, t_k, t_v, g_own, g_par,
    od_own, od_par, d_a, d_b, d_near_a, d_near_b, d_far,
    k_all, v_all, dk_all, dv_all,
):
    tokens = q_own.shape[0]
    col = place[1]
    scale = 1.0 / math.sqrt(q_own.shape[1])
    to_log2 = scale * math.log2(math.e)

    def block(first, which):
        return pl.ds(pl.multiple_of((first + which) * tokens, tokens), tokens)

    at_far = pl.ds(0, tokens)
    at_near_own, at_near_par = block(1, col), block(1, 1 - col)
    at_own, at_par = block(3, col), block(3, 1 - col)
    k_all[at_far] = far[0]
    v_all[at_far] = far[1]
    k_all[at_near_own] = near_own[0]
    v_all[at_near_own] = near_own[1]
    k_all[at_near_par] = near_par[0]
    v_all[at_near_par] = near_par[1]
    k_all[at_own] = k_own[...]
    v_all[at_own] = v_own[...]
    k_all[at_par] = kv_par[0]
    v_all[at_par] = kv_par[1]
    dk_all[...] = jnp.zeros_like(dk_all)
    dv_all[...] = jnp.zeros_like(dv_all)

    def one(q_ref, g_ref, od_ref, first):
        window = pl.ds(pl.multiple_of(first * tokens, tokens), STEPS * tokens)
        q = q_ref[...]
        g = g_ref[...]
        s_t = rows_dot(q, t_k[...])
        s_i = rows_dot(q, k_all[window])
        peak = jnp.maximum(jnp.max(s_t, axis=1, keepdims=True), jnp.max(s_i, axis=1, keepdims=True))
        e_t = jnp.exp2((s_t - peak) * to_log2)
        e_i = jnp.exp2((s_i - peak) * to_log2)
        total = jnp.sum(e_t, axis=1, keepdims=True) + jnp.sum(e_i, axis=1, keepdims=True)
        inverse = 1.0 / total
        p_t = e_t * inverse
        p_i = e_i * inverse
        low_t = p_t.astype(BF16)
        low_i = p_i.astype(BF16)
        out = jnp.dot(low_t, t_v[...], preferred_element_type=F32)
        out += jnp.dot(low_i, v_all[window], preferred_element_type=F32)
        out = out.astype(BF16)
        od_ref[0] = out
        delta = jnp.sum(g.astype(F32) * out.astype(F32), axis=1, keepdims=True)
        ds_t = (p_t * ((rows_dot(g, t_v[...]) - delta) * scale)).astype(BF16)
        ds_i = (p_i * ((rows_dot(g, v_all[window]) - delta) * scale)).astype(BF16)
        dq = jnp.dot(ds_t, t_k[...], preferred_element_type=F32)
        dq += jnp.dot(ds_i, k_all[window], preferred_element_type=F32)
        od_ref[1] = dq.astype(BF16)
        dk_all[window] += cols_dot(ds_i, q)
        dv_all[window] += cols_dot(low_i, g)

    one(q_own, g_own, od_own, col)
    one(q_par, g_par, od_par, 1 - col)
    for place_at, ref in enumerate((d_far, d_near_a, d_near_b, d_a, d_b)):
        rows = pl.ds(place_at * tokens, tokens)
        ref[0] = dk_all[rows].astype(BF16)
        ref[1] = dv_all[rows].astype(BF16)


def attention(place, q, q_par, k, v, kv_par, near_own, near_par, far, t_k, t_v, g_own, g_par):
    tokens = q.shape[0]
    width = q_par.shape[1]
    text = t_k.shape[0]
    heads = width // HEAD_DIM
    whole = lambda rows: pl.BlockSpec((rows, HEAD_DIM), lambda h, place: (0, place[0] * heads + h))
    part = pl.BlockSpec((tokens, HEAD_DIM), lambda h, place: (0, h))
    double = pl.BlockSpec((2, tokens, HEAD_DIM), lambda h, place: (0, 0, h))
    keys = text + STEPS * tokens
    macs = heads * 2 * tokens * HEAD_DIM * (4 * keys + 2 * STEPS * tokens)
    out = jax.ShapeDtypeStruct((2, tokens, width), BF16)
    image_rows = (STEPS + 1) * tokens
    return pl.pallas_call(
        attention_body,
        out_shape=(out,) * 7,
        grid_spec=pltpu.PrefetchScalarGridSpec(
            num_scalar_prefetch=1,
            grid=(heads,),
            in_specs=[whole(tokens), part, whole(tokens), whole(tokens), double, double, double, double,
                      whole(text), whole(text), part, part],
            out_specs=[double] * 7,
            scratch_shapes=[
                pltpu.VMEM((image_rows, HEAD_DIM), BF16),
                pltpu.VMEM((image_rows, HEAD_DIM), BF16),
                pltpu.VMEM((image_rows, HEAD_DIM), F32),
                pltpu.VMEM((image_rows, HEAD_DIM), F32),
            ],
        ),
        compiler_params=pltpu.CompilerParams(vmem_limit_bytes=48 * 1024 * 1024),
        cost_estimate=pl.CostEstimate(
            flops=4 * macs, bytes_accessed=24 * tokens * width * 2, transcendentals=heads * 2 * tokens * keys
        ),
        name="attention",
    )(place, q, q_par, k, v, kv_par, near_own, near_par, far, t_k, t_v, g_own, g_par)


def per_device(image_query, image_key, image_value, text_key, text_value, out_weight, cotangent):
    q, k, v = image_query[0], image_key[0], image_value[0]
    t_k, t_v = text_key[0], text_value[0]
    cot = cotangent[0]
    shards = lax.axis_size("fsdp")
    blocks = lax.axis_size("seq")
    pairs = blocks // 2
    groups = shards // 2
    width = out_weight.shape[0]
    tokens = q.shape[0]
    f, s = lax.axis_index("fsdp"), lax.axis_index("seq")
    col, core, row = s % 2, f % 2, f // 2

    def shift(a, axis, by):
        n = lax.axis_size(axis)
        return lax.ppermute(a, axis, [(i, (i + by) % n) for i in range(n)])

    def swap(a, axis):
        return lax.ppermute(a, axis, [(i, i ^ 1) for i in range(lax.axis_size(axis))])

    shard = [((row + 1 + g) % groups) * 2 + col for g in range(groups)]
    other = [((row + 1 + g) % groups) * 2 + 1 - col for g in range(groups)]

    def after(operands, *others):
        return lax.optimization_barrier((tuple(operands), others))[0]

    every = range(groups)
    last = groups - 1

    def cut(a, index):
        return lax.dynamic_slice_in_dim(a, index * width, width, 1)

    def cut_two(index):
        return jnp.stack([cut(k, index), cut(v, index)])

    half = tokens // 2
    near_own = [shift(cut_two(shard[g]), "seq", 2) for g in every]
    kv_par = [swap(cut_two(other[g]), "seq") for g in every]
    held = [shift(out_weight, "fsdp", -2 * (1 + g)) if g < last else out_weight for g in every]
    cot_par, near_par, far, q_par = [], [], [], []
    for g in every:
        kv, = after([kv_par[g]], near_own[g])
        near_par.append(shift(kv, "seq", 2))
        if g < 2:
            c, = after([cot[g * half : (g + 1) * half]], kv_par[g])
            cot_par.append(swap(c, "seq"))
    for g in every:
        far.append(shift(jnp.where(col == 0, near_par[g], near_own[g]), "seq", 2))
        c, = after([cut(q, other[g])], cot_par[min(g, 1)], *held[:last])
        q_par.append(swap(c, "seq"))
    cot_par = jnp.concatenate(cot_par, axis=0)

    weight = []
    for g in every:
        from_core = swap(held[g], "fsdp")
        weight.append((jnp.where(core == col, held[g], from_core), jnp.where(core == col, from_core, held[g])))

    rows = width // blocks

    def terms_of(od_own, od_par):
        terms = cols_dot(od_own[0], cot) + cols_dot(od_par[0], cot_par)
        terms = terms.reshape(pairs, 2, rows, -1)
        keep = lax.dynamic_index_in_dim(terms, core, 1, keepdims=False)
        give = lax.dynamic_index_in_dim(terms, 1 - core, 1, keepdims=False).astype(BF16)
        return keep, give

    def add(a, b):
        return (a.astype(F32) + b.astype(F32)).astype(BF16)

    def run(g, others):
        g_own = rows_dot(cot, weight[g][0]).astype(BF16)
        g_par = rows_dot(cot_par, weight[g][0]).astype(BF16)
        place = jnp.stack([shard[g], col]).astype(jnp.int32)
        g_own, g_par = after([g_own, g_par], *others)
        return attention(
            place, q, q_par[g], k, v, kv_par[g], near_own[g], near_par[g], far[g], t_k, t_v, g_own, g_par
        )

    own_od, par_od, own_d, total = [], [], [], None
    waited = ()
    for g in every:
        od_own, od_par, d_a, d_b, d_near_a, d_near_b, d_far = run(g, waited)
        own_od.append(od_own)
        if g < last:
            back = shift(d_far, "seq", -2)
            par_od.append(swap(od_par, "seq"))
            keep, give = terms_of(od_own, od_par)
            from_a = shift(d_near_a, "seq", -2)
            from_b = shift(add(d_near_b, back), "seq", -2)
            both = (keep + swap(give, "fsdp").astype(F32)).astype(BF16)
            waited = (back, both)
            both = shift(both, "fsdp", 2 * (1 + g)).astype(F32)
            total = both if total is None else total + both
            sum_a, sum_b = add(d_a, from_a), add(d_b, from_b)
            sum_o, sum_p = jnp.where(col == 0, sum_a, sum_b), jnp.where(col == 0, sum_b, sum_a)
            own_d.append((sum_o, swap(sum_p, "seq")))
        else:
            keep, give = terms_of(*after([od_own, od_par], from_b, total))
            d_far, = after([d_far], from_a)
            back = shift(d_far, "seq", -2)
            par_od.append(swap(od_par, "seq"))
            total = total + keep + swap(give, "fsdp").astype(F32)
            z = s // 2
            mine = lax.dynamic_index_in_dim(total, z, 0, keepdims=False)
            total = total.astype(BF16)
            pieces = []
            for by in range(1, pairs):
                there = lax.dynamic_index_in_dim(total, (z + by) % pairs, 0, keepdims=False)
                pieces.append(shift(there, "seq", 2 * by))
            near_b = add(d_near_b, back)
            from_p = shift(jnp.where(col == 0, near_b, d_near_a), "seq", -2)
            own, = after([jnp.where(col == 0, d_near_a, near_b)], from_p)
            from_o = shift(own, "seq", -2)
            sum_p = add(jnp.where(col == 0, d_b, d_a), from_p)
            par_od = list(after(par_od, from_p))
            for_own = swap(sum_p, "seq")
            from_o, *pieces = after([from_o, *pieces], for_own)
            sum_o = add(jnp.where(col == 0, d_a, d_b), from_o)
            for piece in pieces:
                mine = mine + piece.astype(F32)
            own_d.append((sum_o, for_own))

    rel_out = jnp.concatenate([p for g in range(groups) for p in (own_od[g][0], par_od[g][0])], axis=1)
    rel_weight = jnp.concatenate([p for g in range(groups) for p in weight[g]], axis=0)
    image_out = jnp.dot(rel_out, rel_weight, preferred_element_type=F32).astype(BF16)

    n = blocks * shards

    def mirror(i):
        ss, ff = divmod(i, shards)
        return (ss - ss % 2 + ff % 2) * shards + ff - ff % 2 + ss % 2

    crossed = lax.ppermute(mine.astype(BF16), ("seq", "fsdp"), [(i, mirror(i)) for i in range(n)])
    grad_weight = jnp.where(core == col, mine, crossed.astype(F32))

    def assemble(pieces):
        whole = jnp.zeros((tokens, width * shards), BF16)
        for g in range(groups):
            whole = lax.dynamic_update_slice_in_dim(whole, pieces[g][0], shard[g] * width, 1)
            whole = lax.dynamic_update_slice_in_dim(whole, pieces[g][1], other[g] * width, 1)
        return whole

    grad_q = assemble([(own_od[g][1], par_od[g][1]) for g in range(groups)])
    grad_k = assemble([(own_d[g][0][0], own_d[g][1][0]) for g in range(groups)])
    grad_v = assemble([(own_d[g][0][1], own_d[g][1][1]) for g in range(groups)])
    return image_out[None], grad_q[None], grad_k[None], grad_v[None], grad_weight


def solution(mesh):
    in_specs = (
        P("fsdp", "seq", None),
        P("fsdp", "seq", None),
        P("fsdp", "seq", None),
        P("fsdp", None, None),
        P("fsdp", None, None),
        P("fsdp", None),
        P("fsdp", "seq", None),
    )
    out_specs = (
        P("fsdp", "seq", None),
        P("fsdp", "seq", None),
        P("fsdp", "seq", None),
        P("fsdp", "seq", None),
        P(("fsdp", "seq"), None),
    )
    return jax.shard_map(
        per_device, mesh=mesh, in_specs=in_specs, out_specs=out_specs, check_vma=False
    )
```

```python
import functools
import math

import jax
import jax.numpy as jnp
from jax import lax
from jax.experimental import pallas as pl
from jax.experimental.pallas import tpu as pltpu
from jax.sharding import PartitionSpec as P

HEAD_DIM = 128
STEPS = 4
F32 = jnp.float32
BF16 = jnp.bfloat16


def rows_dot(a, b):
    return lax.dot_general(a, b, (((1,), (1,)), ((), ())), preferred_element_type=F32)


def cols_dot(a, b):
    return lax.dot_general(a, b, (((0,), (0,)), ((), ())), preferred_element_type=F32)


def dot(a, b):
    return jnp.dot(a, b, preferred_element_type=F32)


def attention_body(
    place, q_own, q_par, k_own, v_own, kv_par, near_own, near_par, far, t_k, t_v, g_own, g_par,
    od_own, od_par, d_a, d_b, d_near_a, d_near_b, d_far,
):
    tokens = q_own.shape[0]
    first = place[1] == 0
    scale = 1.0 / math.sqrt(q_own.shape[1])
    to_log2 = scale * math.log2(math.e)

    def by_block(own, par):
        return jnp.where(first, own, par), jnp.where(first, par, own)

    q = by_block(q_own[...], q_par[...])
    g = by_block(g_own[...], g_par[...])
    text = t_k.shape[0] // tokens
    keys = [t_k[i * tokens : (i + 1) * tokens] for i in range(text)]
    keys += [far[0], *by_block(near_own[0], near_par[0]), *by_block(k_own[...], kv_par[0])]
    values = [t_v[i * tokens : (i + 1) * tokens] for i in range(text)]
    values += [far[1], *by_block(near_own[1], near_par[1]), *by_block(v_own[...], kv_par[1])]
    keys_t = [k.T for k in keys]
    values_t = [v.T for v in values]
    sets = [list(range(text)) + list(range(text + i, text + i + STEPS)) for i in range(2)]
    score = [{j: rows_dot(keys[j], q[i]) for j in sets[i]} for i in range(2)]
    prob, low, grad_low = [], [], []
    out_t = []
    for i in range(2):
        peak = functools.reduce(jnp.maximum, [score[i][j] for j in sets[i]])
        peak = jnp.max(peak, axis=0, keepdims=True)
        e = {j: jnp.exp2((score[i][j] - peak) * to_log2) for j in sets[i]}
        total = jnp.sum(functools.reduce(jnp.add, e.values()), axis=0, keepdims=True)
        inverse = 1.0 / total
        prob.append({j: e[j] * inverse for j in sets[i]})
        low.append({j: prob[i][j].astype(BF16) for j in sets[i]})
        out_t.append(functools.reduce(jnp.add, [dot(values_t[j], low[i][j]) for j in sets[i]]))
    outs, dqs = [], []
    for i in range(2):
        out = out_t[i].T.astype(BF16)
        outs.append(out)
        delta = jnp.sum(g[i].T.astype(F32) * out_t[i].astype(BF16).astype(F32), axis=0, keepdims=True)
        grad_low.append({
            j: (prob[i][j] * (rows_dot(values[j], g[i]) - delta)).astype(BF16) for j in sets[i]
        })
        dq = functools.reduce(jnp.add, [dot(keys_t[j], grad_low[i][j]) for j in sets[i]])
        dqs.append((dq * scale).T.astype(BF16))
    for n, (own, par) in enumerate((by_block(*outs), by_block(*dqs))):
        od_own[n] = own
        od_par[n] = par
    for n, ref in enumerate((d_far, d_near_a, d_near_b, d_a, d_b)):
        j = text + n
        users = [i for i in range(2) if j in sets[i]]
        dk = functools.reduce(jnp.add, [dot(grad_low[i][j], q[i]) for i in users])
        dv = functools.reduce(jnp.add, [dot(low[i][j], g[i]) for i in users])
        ref[0] = (dk * scale).astype(BF16)
        ref[1] = dv.astype(BF16)


def attention(place, q, q_par, k, v, kv_par, near_own, near_par, far, t_k, t_v, g_own, g_par):
    tokens = q.shape[0]
    width = q_par.shape[1]
    text = t_k.shape[0]
    heads = width // HEAD_DIM
    whole = lambda rows: pl.BlockSpec((rows, HEAD_DIM), lambda h, place: (0, place[0] * heads + h))
    part = pl.BlockSpec((tokens, HEAD_DIM), lambda h, place: (0, h))
    double = pl.BlockSpec((2, tokens, HEAD_DIM), lambda h, place: (0, 0, h))
    keys = text + STEPS * tokens
    macs = heads * 2 * tokens * HEAD_DIM * (4 * keys + 2 * STEPS * tokens)
    out = jax.ShapeDtypeStruct((2, tokens, width), BF16)
    return pl.pallas_call(
        attention_body,
        out_shape=(out,) * 7,
        grid_spec=pltpu.PrefetchScalarGridSpec(
            num_scalar_prefetch=1,
            grid=(heads,),
            in_specs=[whole(tokens), part, whole(tokens), whole(tokens), double, double, double, double,
                      whole(text), whole(text), part, part],
            out_specs=[double] * 7,
        ),
        compiler_params=pltpu.CompilerParams(vmem_limit_bytes=48 * 1024 * 1024),
        cost_estimate=pl.CostEstimate(
            flops=4 * macs, bytes_accessed=24 * tokens * width * 2, transcendentals=heads * 2 * tokens * keys
        ),
        name="attention",
    )(place, q, q_par, k, v, kv_par, near_own, near_par, far, t_k, t_v, g_own, g_par)


def per_device(image_query, image_key, image_value, text_key, text_value, out_weight, cotangent):
    q, k, v = image_query[0], image_key[0], image_value[0]
    t_k, t_v = text_key[0], text_value[0]
    cot = cotangent[0]
    shards = lax.axis_size("fsdp")
    blocks = lax.axis_size("seq")
    pairs = blocks // 2
    groups = shards // 2
    width = out_weight.shape[0]
    tokens = q.shape[0]
    f, s = lax.axis_index("fsdp"), lax.axis_index("seq")
    col, core, row = s % 2, f % 2, f // 2

    def shift(a, axis, by):
        n = lax.axis_size(axis)
        return lax.ppermute(a, axis, [(i, (i + by) % n) for i in range(n)])

    def swap(a, axis):
        return lax.ppermute(a, axis, [(i, i ^ 1) for i in range(lax.axis_size(axis))])

    shard = [((row + 1 + g) % groups) * 2 + col for g in range(groups)]
    other = [((row + 1 + g) % groups) * 2 + 1 - col for g in range(groups)]

    def after(operands, *others):
        return lax.optimization_barrier((tuple(operands), others))[0]

    every = range(groups)
    last = groups - 1

    def cut(a, index):
        return lax.dynamic_slice_in_dim(a, index * width, width, 1)

    def cut_two(index):
        return jnp.stack([cut(k, index), cut(v, index)])

    half = tokens // 2
    kv_own = [cut_two(shard[g]) for g in every]
    near_own = [shift(kv_own[g], "seq", 2) for g in every]
    kv_par = [swap(cut_two(other[g]), "seq") for g in every]
    held = [shift(out_weight, "fsdp", -2 * (1 + g)) if g < last else out_weight for g in every]
    cot_par, near_par, far, q_par = [], [], [], []
    for g in every:
        kv, = after([kv_par[g]], near_own[g])
        near_par.append(shift(kv, "seq", 2))
        if g < 2:
            c, = after([cot[g * half : (g + 1) * half]], kv_par[g], near_own[g])
            cot_par.append(swap(c, "seq"))
    for g in every:
        b_near = jnp.where(col == 0, near_par[g], near_own[g])
        far.append(shift(b_near, "seq", 2))
        c, = after([cut(q, other[g])], cot_par[min(g, 1)], *held[:last])
        q_par.append(swap(c, "seq"))
    cot_par = jnp.concatenate(cot_par, axis=0)

    weight = []
    for g in every:
        from_core = swap(held[g], "fsdp")
        weight.append((jnp.where(core == col, held[g], from_core), jnp.where(core == col, from_core, held[g])))

    rows = width // blocks

    def terms_of(od_own, od_par):
        terms = cols_dot(od_own[0], cot) + cols_dot(od_par[0], cot_par)
        terms = terms.reshape(pairs, 2, rows, -1)
        keep = lax.dynamic_index_in_dim(terms, core, 1, keepdims=False)
        give = lax.dynamic_index_in_dim(terms, 1 - core, 1, keepdims=False).astype(BF16)
        return keep, give

    def add(a, b):
        return (a.astype(F32) + b.astype(F32)).astype(BF16)

    def run(g, others):
        g_own = rows_dot(cot, weight[g][0]).astype(BF16)
        g_par = rows_dot(cot_par, weight[g][0]).astype(BF16)
        place = jnp.stack([shard[g], col]).astype(jnp.int32)
        g_own, g_par = after([g_own, g_par], *others)
        return attention(
            place, q, q_par[g], k, v, kv_par[g], near_own[g], near_par[g], far[g], t_k, t_v, g_own, g_par
        )

    own_od, par_od, own_d, total = [], [], [], None
    waited = ()
    for g in every:
        od_own, od_par, d_a, d_b, d_near_a, d_near_b, d_far = run(g, waited)
        own_od.append(od_own)
        if g < last:
            back = shift(d_far, "seq", -2)
            od_p, = after([od_par], back)
            par_od.append(swap(od_p, "seq"))
            keep, give = terms_of(od_own, od_par)
            from_a = shift(d_near_a, "seq", -2)
            from_b = shift(add(d_near_b, back), "seq", -2)
            both = (keep + swap(give, "fsdp").astype(F32)).astype(BF16)
            waited = (back, both)
            both = shift(both, "fsdp", 2 * (1 + g)).astype(F32)
            total = both if total is None else total + both
            sum_a, sum_b = add(d_a, from_a), add(d_b, from_b)
            sum_o, sum_p = jnp.where(col == 0, sum_a, sum_b), jnp.where(col == 0, sum_b, sum_a)
            own_d.append((sum_o, swap(sum_p, "seq")))
        else:
            keep, give = terms_of(od_own, od_par)
            d_far, = after([d_far], from_a)
            back = shift(d_far, "seq", -2)
            od_par, = after([od_par], from_b)
            par_od.append(swap(od_par, "seq"))
            total = total + keep + swap(give, "fsdp").astype(F32)
            z = s // 2
            mine = lax.dynamic_index_in_dim(total, z, 0, keepdims=False)
            total = total.astype(BF16)
            total, = after([total], back)
            pieces = []
            for by in range(1, pairs):
                there = lax.dynamic_index_in_dim(total, (z + by) % pairs, 0, keepdims=False)
                pieces.append(shift(there, "seq", 2 * by))
            near_b = add(d_near_b, back)
            from_p = shift(jnp.where(col == 0, near_b, d_near_a), "seq", -2)
            own = jnp.where(col == 0, d_near_a, near_b)
            own, = after([own], *pieces)
            from_o = shift(own, "seq", -2)
            sum_p = add(jnp.where(col == 0, d_b, d_a), from_p)
            par_od = list(after(par_od, from_p))
            own_d = [(a, *after([b], from_p)) for a, b in own_d]
            for_own = swap(sum_p, "seq")
            for piece in pieces:
                mine = mine + piece.astype(F32)
            n = blocks * shards

            def mirror(i):
                ss, ff = divmod(i, shards)
                return (ss - ss % 2 + ff % 2) * shards + ff - ff % 2 + ss % 2

            crossed = lax.ppermute(mine.astype(BF16), ("seq", "fsdp"), [(i, mirror(i)) for i in range(n)])
            grad_weight = jnp.where(core == col, mine, crossed.astype(F32))
            from_o, = after([from_o], for_own, grad_weight)
            sum_o = add(jnp.where(col == 0, d_a, d_b), from_o)
            own_d.append((sum_o, for_own))

    rel_out = jnp.concatenate([p for g in range(groups) for p in (own_od[g][0], par_od[g][0])], axis=1)
    rel_weight = jnp.concatenate([p for g in range(groups) for p in weight[g]], axis=0)
    image_out = jnp.dot(rel_out, rel_weight, preferred_element_type=F32).astype(BF16)

    def assemble(pieces):
        whole = jnp.zeros((tokens, width * shards), BF16)
        for g in range(groups):
            whole = lax.dynamic_update_slice_in_dim(whole, pieces[g][0], shard[g] * width, 1)
            whole = lax.dynamic_update_slice_in_dim(whole, pieces[g][1], other[g] * width, 1)
        return whole

    grad_q = assemble([(own_od[g][1], par_od[g][1]) for g in range(groups)])
    grad_k = assemble([(own_d[g][0][0], own_d[g][1][0]) for g in range(groups)])
    grad_v = assemble([(own_d[g][0][1], own_d[g][1][1]) for g in range(groups)])
    return image_out[None], grad_q[None], grad_k[None], grad_v[None], grad_weight


def solution(mesh):
    in_specs = (
        P("fsdp", "seq", None),
        P("fsdp", "seq", None),
        P("fsdp", "seq", None),
        P("fsdp", None, None),
        P("fsdp", None, None),
        P("fsdp", None),
        P("fsdp", "seq", None),
    )
    out_specs = (
        P("fsdp", "seq", None),
        P("fsdp", "seq", None),
        P("fsdp", "seq", None),
        P("fsdp", "seq", None),
        P(("fsdp", "seq"), None),
    )
    return jax.shard_map(
        per_device, mesh=mesh, in_specs=in_specs, out_specs=out_specs, check_vma=False
    )
```

```python
import functools
import math

import jax
import jax.numpy as jnp
from jax import lax
from jax.experimental import pallas as pl
from jax.experimental.pallas import tpu as pltpu
from jax.sharding import PartitionSpec as P

HEAD_DIM = 128
STEPS = 4
F32 = jnp.float32
BF16 = jnp.bfloat16


def rows_dot(a, b):
    return lax.dot_general(a, b, (((1,), (1,)), ((), ())), preferred_element_type=F32)


def cols_dot(a, b):
    return lax.dot_general(a, b, (((0,), (0,)), ((), ())), preferred_element_type=F32)


def dot(a, b):
    return jnp.dot(a, b, preferred_element_type=F32)


def attention_body(
    place, q_own, q_par, k_own, v_own, kv_par, near_own, near_par, far, t_k, t_v, g_own, g_par,
    od_own, od_par, d_a, d_b, d_near_a, d_near_b, d_far,
):
    tokens = q_own.shape[0]
    first = place[1] == 0
    scale = 1.0 / math.sqrt(q_own.shape[1])
    to_log2 = scale * math.log2(math.e)

    def by_block(own, par):
        return jnp.where(first, own, par), jnp.where(first, par, own)

    q = by_block(q_own[...], q_par[...])
    g = by_block(g_own[...], g_par[...])
    text = t_k.shape[0] // tokens
    keys = [t_k[i * tokens : (i + 1) * tokens] for i in range(text)]
    keys += [far[0], *by_block(near_own[0], near_par[0]), *by_block(k_own[...], kv_par[0])]
    values = [t_v[i * tokens : (i + 1) * tokens] for i in range(text)]
    values += [far[1], *by_block(near_own[1], near_par[1]), *by_block(v_own[...], kv_par[1])]
    keys_t = [k.T for k in keys]
    values_t = [v.T for v in values]
    sets = [list(range(text)) + list(range(text + i, text + i + STEPS)) for i in range(2)]
    score = [{j: rows_dot(keys[j], q[i]) for j in sets[i]} for i in range(2)]
    prob, low, grad_low = [], [], []
    out_t = []
    for i in range(2):
        peak = functools.reduce(jnp.maximum, [score[i][j] for j in sets[i]])
        peak = jnp.max(peak, axis=0, keepdims=True)
        e = {j: jnp.exp2((score[i][j] - peak) * to_log2) for j in sets[i]}
        total = jnp.sum(functools.reduce(jnp.add, e.values()), axis=0, keepdims=True)
        inverse = 1.0 / total
        prob.append({j: e[j] * inverse for j in sets[i]})
        low.append({j: prob[i][j].astype(BF16) for j in sets[i]})
        out_t.append(functools.reduce(jnp.add, [dot(values_t[j], low[i][j]) for j in sets[i]]))
    outs, dqs = [], []
    for i in range(2):
        out = out_t[i].T.astype(BF16)
        outs.append(out)
        delta = jnp.sum(g[i].T.astype(F32) * out_t[i].astype(BF16).astype(F32), axis=0, keepdims=True)
        grad_low.append({
            j: (prob[i][j] * (rows_dot(values[j], g[i]) - delta)).astype(BF16) for j in sets[i]
        })
        dq = functools.reduce(jnp.add, [dot(keys_t[j], grad_low[i][j]) for j in sets[i]])
        dqs.append((dq * scale).T.astype(BF16))
    for n, (own, par) in enumerate((by_block(*outs), by_block(*dqs))):
        od_own[n] = own
        od_par[n] = par
    for n, ref in enumerate((d_far, d_near_a, d_near_b, d_a, d_b)):
        j = text + n
        users = [i for i in range(2) if j in sets[i]]
        dk = functools.reduce(jnp.add, [dot(grad_low[i][j], q[i]) for i in users])
        dv = functools.reduce(jnp.add, [dot(low[i][j], g[i]) for i in users])
        ref[0] = (dk * scale).astype(BF16)
        ref[1] = dv.astype(BF16)


def attention(place, q, q_par, k, v, kv_par, near_own, near_par, far, t_k, t_v, g_own, g_par):
    tokens = q.shape[0]
    width = q_par.shape[1]
    text = t_k.shape[0]
    heads = width // HEAD_DIM
    whole = lambda rows: pl.BlockSpec((rows, HEAD_DIM), lambda h, place: (0, place[0] * heads + h))
    part = pl.BlockSpec((tokens, HEAD_DIM), lambda h, place: (0, h))
    double = pl.BlockSpec((2, tokens, HEAD_DIM), lambda h, place: (0, 0, h))
    keys = text + STEPS * tokens
    macs = heads * 2 * tokens * HEAD_DIM * (4 * keys + 2 * STEPS * tokens)
    out = jax.ShapeDtypeStruct((2, tokens, width), BF16)
    return pl.pallas_call(
        attention_body,
        out_shape=(out,) * 7,
        grid_spec=pltpu.PrefetchScalarGridSpec(
            num_scalar_prefetch=1,
            grid=(heads,),
            in_specs=[whole(tokens), part, whole(tokens), whole(tokens), double, double, double, double,
                      whole(text), whole(text), part, part],
            out_specs=[double] * 7,
        ),
        compiler_params=pltpu.CompilerParams(vmem_limit_bytes=16 * 1024 * 1024),
        cost_estimate=pl.CostEstimate(
            flops=4 * macs, bytes_accessed=24 * tokens * width * 2, transcendentals=heads * 2 * tokens * keys
        ),
        name="attention",
    )(place, q, q_par, k, v, kv_par, near_own, near_par, far, t_k, t_v, g_own, g_par)


def per_device(image_query, image_key, image_value, text_key, text_value, out_weight, cotangent):
    q, k, v = image_query[0], image_key[0], image_value[0]
    t_k, t_v = text_key[0], text_value[0]
    cot = cotangent[0]
    shards = lax.axis_size("fsdp")
    blocks = lax.axis_size("seq")
    pairs = blocks // 2
    groups = shards // 2
    width = out_weight.shape[0]
    tokens = q.shape[0]
    f, s = lax.axis_index("fsdp"), lax.axis_index("seq")
    col, core, row = s % 2, f % 2, f // 2

    def shift(a, axis, by):
        n = lax.axis_size(axis)
        return lax.ppermute(a, axis, [(i, (i + by) % n) for i in range(n)])

    def swap(a, axis):
        return lax.ppermute(a, axis, [(i, i ^ 1) for i in range(lax.axis_size(axis))])

    shard = [((row + 1 + g) % groups) * 2 + col for g in range(groups)]
    other = [((row + 1 + g) % groups) * 2 + 1 - col for g in range(groups)]

    def after(operands, *others):
        return lax.optimization_barrier((tuple(operands), others))[0]

    every = range(groups)
    last = groups - 1

    def cut(a, index):
        return lax.dynamic_slice_in_dim(a, index * width, width, 1)

    def cut_two(index):
        return jnp.stack([cut(k, index), cut(v, index)])

    half = tokens // 2
    kv_own = [cut_two(shard[g]) for g in every]
    near_own = [shift(kv_own[g], "seq", 2) for g in every]
    kv_par = [swap(cut_two(other[g]), "seq") for g in every]
    held = [shift(out_weight, "fsdp", -2 * (1 + g)) if g < last else out_weight for g in every]
    cot_par, near_par, far, q_par = [], [], [], []
    for g in every:
        kv, = after([kv_par[g]], near_own[g])
        near_par.append(shift(kv, "seq", 2))
        if g < 2:
            c, = after([cot[g * half : (g + 1) * half]], kv_par[g])
            cot_par.append(swap(c, "seq"))
    for g in every:
        b_near = jnp.where(col == 0, near_par[g], near_own[g])
        far.append(shift(b_near, "seq", 2))
        c, = after([cut(q, other[g])], cot_par[min(g, len(cot_par) - 1)])
        q_par.append(swap(c, "seq"))
    cot_par = jnp.concatenate(cot_par, axis=0)

    weight = []
    for g in every:
        from_core = swap(held[g], "fsdp")
        weight.append((jnp.where(core == col, held[g], from_core), jnp.where(core == col, from_core, held[g])))

    rows = width // blocks

    def terms_of(od_own, od_par):
        terms = cols_dot(od_own[0], cot) + cols_dot(od_par[0], cot_par)
        terms = terms.reshape(pairs, 2, rows, -1)
        keep = lax.dynamic_index_in_dim(terms, core, 1, keepdims=False)
        give = lax.dynamic_index_in_dim(terms, 1 - core, 1, keepdims=False).astype(BF16)
        return keep, give

    def add(a, b):
        return (a.astype(F32) + b.astype(F32)).astype(BF16)

    def run(g, others):
        g_own = rows_dot(cot, weight[g][0]).astype(BF16)
        g_par = rows_dot(cot_par, weight[g][0]).astype(BF16)
        place = jnp.stack([shard[g], col]).astype(jnp.int32)
        g_own, g_par = after([g_own, g_par], *others)
        return attention(
            place, q, q_par[g], k, v, kv_par[g], near_own[g], near_par[g], far[g], t_k, t_v, g_own, g_par
        )

    own_od, par_od, own_d, total = [], [], [], None
    waited = ()
    for g in every:
        od_own, od_par, d_a, d_b, d_near_a, d_near_b, d_far = run(g, waited)
        own_od.append(od_own)
        if g < last:
            back = shift(d_far, "seq", -2)
            od_p, = after([od_par], back)
            par_od.append(swap(od_p, "seq"))
            keep, give = terms_of(od_own, od_par)
            from_a = shift(d_near_a, "seq", -2)
            from_b = shift(add(d_near_b, back), "seq", -2)
            both = (keep + swap(give, "fsdp").astype(F32)).astype(BF16)
            waited = (back, both)
            both = shift(both, "fsdp", 2 * (1 + g)).astype(F32)
            total = both if total is None else total + both
            sum_a, sum_b = add(d_a, from_a), add(d_b, from_b)
            sum_o, sum_p = jnp.where(col == 0, sum_a, sum_b), jnp.where(col == 0, sum_b, sum_a)
            own_d.append((sum_o, swap(sum_p, "seq")))
        else:
            keep, give = terms_of(od_own, od_par)
            d_far, = after([d_far], from_a)
            back = shift(d_far, "seq", -2)
            od_par, = after([od_par], from_b, total)
            par_od.append(swap(od_par, "seq"))
            total = total + keep + swap(give, "fsdp").astype(F32)
            z = s // 2
            mine = lax.dynamic_index_in_dim(total, z, 0, keepdims=False)
            total = total.astype(BF16)
            total, = after([total], back)
            pieces = []
            for by in range(1, pairs):
                there = lax.dynamic_index_in_dim(total, (z + by) % pairs, 0, keepdims=False)
                pieces.append(shift(there, "seq", 2 * by))
            near_b = add(d_near_b, back)
            from_p = shift(jnp.where(col == 0, near_b, d_near_a), "seq", -2)
            sum_p = add(jnp.where(col == 0, d_b, d_a), from_p)
            par_od = list(after(par_od, from_p))
            own_d = [(a, *after([b], from_p)) for a, b in own_d]
            for_own = swap(sum_p, "seq")
            for piece in pieces:
                mine = mine + piece.astype(F32)
            n = blocks * shards

            def mirror(i):
                ss, ff = divmod(i, shards)
                return (ss - ss % 2 + ff % 2) * shards + ff - ff % 2 + ss % 2

            crossed = lax.ppermute(mine.astype(BF16), ("seq", "fsdp"), [(i, mirror(i)) for i in range(n)])
            grad_weight = jnp.where(core == col, mine, crossed.astype(F32))
            own = jnp.where(col == 0, d_near_a, near_b)
            own, = after([own], *pieces)
            from_o = shift(own, "seq", -2)
            from_o, = after([from_o], for_own, grad_weight)
            sum_o = add(jnp.where(col == 0, d_a, d_b), from_o)
            own_d.append((sum_o, for_own))

    rel_out = jnp.concatenate([p for g in range(groups) for p in (own_od[g][0], par_od[g][0])], axis=1)
    rel_weight = jnp.concatenate([p for g in range(groups) for p in weight[g]], axis=0)
    image_out = jnp.dot(rel_out, rel_weight, preferred_element_type=F32).astype(BF16)

    def assemble(pieces):
        whole = jnp.zeros((tokens, width * shards), BF16)
        for g in range(groups):
            whole = lax.dynamic_update_slice_in_dim(whole, pieces[g][0], shard[g] * width, 1)
            whole = lax.dynamic_update_slice_in_dim(whole, pieces[g][1], other[g] * width, 1)
        return whole

    grad_q = assemble([(own_od[g][1], par_od[g][1]) for g in range(groups)])
    grad_k = assemble([(own_d[g][0][0], own_d[g][1][0]) for g in range(groups)])
    grad_v = assemble([(own_d[g][0][1], own_d[g][1][1]) for g in range(groups)])
    return image_out[None], grad_q[None], grad_k[None], grad_v[None], grad_weight


def solution(mesh):
    in_specs = (
        P("fsdp", "seq", None),
        P("fsdp", "seq", None),
        P("fsdp", "seq", None),
        P("fsdp", None, None),
        P("fsdp", None, None),
        P("fsdp", None),
        P("fsdp", "seq", None),
    )
    out_specs = (
        P("fsdp", "seq", None),
        P("fsdp", "seq", None),
        P("fsdp", "seq", None),
        P("fsdp", "seq", None),
        P(("fsdp", "seq"), None),
    )
    return jax.shard_map(
        per_device, mesh=mesh, in_specs=in_specs, out_specs=out_specs, check_vma=False
    )
```

```python
import functools
import math

import jax
import jax.numpy as jnp
from jax import lax
from jax.experimental import pallas as pl
from jax.experimental.pallas import tpu as pltpu
from jax.sharding import PartitionSpec as P

HEAD_DIM = 128
STEPS = 4
F32 = jnp.float32
BF16 = jnp.bfloat16


def rows_dot(a, b):
    return lax.dot_general(a, b, (((1,), (1,)), ((), ())), preferred_element_type=F32)


def cols_dot(a, b):
    return lax.dot_general(a, b, (((0,), (0,)), ((), ())), preferred_element_type=F32)


def dot(a, b):
    return jnp.dot(a, b, preferred_element_type=F32)


def attention_body(
    place, q_own, q_par, k_own, v_own, kv_par, near_own, near_par, far, t_k, t_v, g_own, g_par,
    od_own, od_par, d_a, d_b, d_near_a, d_near_b, d_far,
):
    tokens = q_own.shape[0]
    first = place[1] == 0
    scale = 1.0 / math.sqrt(q_own.shape[1])
    to_log2 = scale * math.log2(math.e)

    def by_block(own, par):
        return jnp.where(first, own, par), jnp.where(first, par, own)

    q = by_block(q_own[...], q_par[...])
    g = by_block(g_own[...], g_par[...])
    text = t_k.shape[0] // tokens
    keys = [t_k[i * tokens : (i + 1) * tokens] for i in range(text)]
    keys += [far[0], *by_block(near_own[0], near_par[0]), *by_block(k_own[...], kv_par[0])]
    values = [t_v[i * tokens : (i + 1) * tokens] for i in range(text)]
    values += [far[1], *by_block(near_own[1], near_par[1]), *by_block(v_own[...], kv_par[1])]
    keys_t = [k.T for k in keys]
    values_t = [v.T for v in values]
    sets = [list(range(text)) + list(range(text + i, text + i + STEPS)) for i in range(2)]
    score = [{j: rows_dot(keys[j], q[i]) for j in sets[i]} for i in range(2)]
    prob, low, grad_low = [], [], []
    out_t = []
    for i in range(2):
        peak = functools.reduce(jnp.maximum, [score[i][j] for j in sets[i]])
        peak = jnp.max(peak, axis=0, keepdims=True)
        e = {j: jnp.exp2((score[i][j] - peak) * to_log2) for j in sets[i]}
        total = jnp.sum(functools.reduce(jnp.add, e.values()), axis=0, keepdims=True)
        inverse = 1.0 / total
        prob.append({j: e[j] * inverse for j in sets[i]})
        low.append({j: prob[i][j].astype(BF16) for j in sets[i]})
        out_t.append(dot(jnp.concatenate([values_t[j] for j in sets[i]], axis=1), jnp.concatenate([low[i][j] for j in sets[i]], axis=0)))
    outs, dqs = [], []
    for i in range(2):
        out = out_t[i].T.astype(BF16)
        outs.append(out)
        delta = jnp.sum(g[i].T.astype(F32) * out_t[i].astype(BF16).astype(F32), axis=0, keepdims=True)
        grad_low.append({
            j: (prob[i][j] * (rows_dot(values[j], g[i]) - delta)).astype(BF16) for j in sets[i]
        })
        dq = dot(jnp.concatenate([keys_t[j] for j in sets[i]], axis=1), jnp.concatenate([grad_low[i][j] for j in sets[i]], axis=0))
        dqs.append((dq * scale).T.astype(BF16))
    for n, (own, par) in enumerate((by_block(*outs), by_block(*dqs))):
        od_own[n] = own
        od_par[n] = par
    for n, ref in enumerate((d_far, d_near_a, d_near_b, d_a, d_b)):
        j = text + n
        users = [i for i in range(2) if j in sets[i]]
        dk = functools.reduce(jnp.add, [dot(grad_low[i][j], q[i]) for i in users])
        dv = functools.reduce(jnp.add, [dot(low[i][j], g[i]) for i in users])
        ref[0] = (dk * scale).astype(BF16)
        ref[1] = dv.astype(BF16)


def attention(place, q, q_par, k, v, kv_par, near_own, near_par, far, t_k, t_v, g_own, g_par):
    tokens = q.shape[0]
    width = q_par.shape[1]
    text = t_k.shape[0]
    heads = width // HEAD_DIM
    whole = lambda rows: pl.BlockSpec((rows, HEAD_DIM), lambda h, place: (0, place[0] * heads + h))
    part = pl.BlockSpec((tokens, HEAD_DIM), lambda h, place: (0, h))
    double = pl.BlockSpec((2, tokens, HEAD_DIM), lambda h, place: (0, 0, h))
    keys = text + STEPS * tokens
    macs = heads * 2 * tokens * HEAD_DIM * (4 * keys + 2 * STEPS * tokens)
    out = jax.ShapeDtypeStruct((2, tokens, width), BF16)
    return pl.pallas_call(
        attention_body,
        out_shape=(out,) * 7,
        grid_spec=pltpu.PrefetchScalarGridSpec(
            num_scalar_prefetch=1,
            grid=(heads,),
            in_specs=[whole(tokens), part, whole(tokens), whole(tokens), double, double, double, double,
                      whole(text), whole(text), part, part],
            out_specs=[double] * 7,
        ),
        compiler_params=pltpu.CompilerParams(vmem_limit_bytes=16 * 1024 * 1024),
        cost_estimate=pl.CostEstimate(
            flops=4 * macs, bytes_accessed=24 * tokens * width * 2, transcendentals=heads * 2 * tokens * keys
        ),
        name="attention",
    )(place, q, q_par, k, v, kv_par, near_own, near_par, far, t_k, t_v, g_own, g_par)


def per_device(image_query, image_key, image_value, text_key, text_value, out_weight, cotangent):
    q, k, v = image_query[0], image_key[0], image_value[0]
    t_k, t_v = text_key[0], text_value[0]
    cot = cotangent[0]
    shards = lax.axis_size("fsdp")
    blocks = lax.axis_size("seq")
    pairs = blocks // 2
    groups = shards // 2
    width = out_weight.shape[0]
    tokens = q.shape[0]
    f, s = lax.axis_index("fsdp"), lax.axis_index("seq")
    col, core, row = s % 2, f % 2, f // 2

    def shift(a, axis, by):
        n = lax.axis_size(axis)
        return lax.ppermute(a, axis, [(i, (i + by) % n) for i in range(n)])

    def swap(a, axis):
        return lax.ppermute(a, axis, [(i, i ^ 1) for i in range(lax.axis_size(axis))])

    shard = [((row + 1 + g) % groups) * 2 + col for g in range(groups)]
    other = [((row + 1 + g) % groups) * 2 + 1 - col for g in range(groups)]

    def after(operands, *others):
        return lax.optimization_barrier((tuple(operands), others))[0]

    every = range(groups)
    last = groups - 1

    def cut(a, index):
        return lax.dynamic_slice_in_dim(a, index * width, width, 1)

    def cut_two(index):
        return jnp.stack([cut(k, index), cut(v, index)])

    half = tokens // 2
    kv_own = [cut_two(shard[g]) for g in every]
    near_own = [shift(kv_own[g], "seq", 2) for g in every]
    kv_par = [swap(cut_two(other[g]), "seq") for g in every]
    held = [shift(out_weight, "fsdp", -2 * (1 + g)) if g < last else out_weight for g in every]
    cot_par, near_par, far, q_par = [], [], [], []
    for g in every:
        kv, = after([kv_par[g]], near_own[g])
        near_par.append(shift(kv, "seq", 2))
        if g < 2:
            c, = after([cot[g * half : (g + 1) * half]], kv_par[g])
            cot_par.append(swap(c, "seq"))
    for g in every:
        b_near = jnp.where(col == 0, near_par[g], near_own[g])
        far.append(shift(b_near, "seq", 2))
        c, = after([cut(q, other[g])], cot_par[min(g, len(cot_par) - 1)])
        q_par.append(swap(c, "seq"))
    cot_par = jnp.concatenate(cot_par, axis=0)

    weight = []
    for g in every:
        from_core = swap(held[g], "fsdp")
        weight.append((jnp.where(core == col, held[g], from_core), jnp.where(core == col, from_core, held[g])))

    rows = width // blocks

    def terms_of(od_own, od_par):
        terms = cols_dot(od_own[0], cot) + cols_dot(od_par[0], cot_par)
        terms = terms.reshape(pairs, 2, rows, -1)
        keep = lax.dynamic_index_in_dim(terms, core, 1, keepdims=False)
        give = lax.dynamic_index_in_dim(terms, 1 - core, 1, keepdims=False).astype(BF16)
        return keep, give

    def add(a, b):
        return (a.astype(F32) + b.astype(F32)).astype(BF16)

    def run(g, others):
        g_own = rows_dot(cot, weight[g][0]).astype(BF16)
        g_par = rows_dot(cot_par, weight[g][0]).astype(BF16)
        place = jnp.stack([shard[g], col]).astype(jnp.int32)
        g_own, g_par = after([g_own, g_par], *others)
        return attention(
            place, q, q_par[g], k, v, kv_par[g], near_own[g], near_par[g], far[g], t_k, t_v, g_own, g_par
        )

    own_od, par_od, own_d, total = [], [], [], None
    waited = ()
    for g in every:
        od_own, od_par, d_a, d_b, d_near_a, d_near_b, d_far = run(g, waited)
        own_od.append(od_own)
        if g < last:
            back = shift(d_far, "seq", -2)
            od_p, = after([od_par], back)
            par_od.append(swap(od_p, "seq"))
            keep, give = terms_of(od_own, od_par)
            from_a = shift(d_near_a, "seq", -2)
            from_b = shift(add(d_near_b, back), "seq", -2)
            both = (keep + swap(give, "fsdp").astype(F32)).astype(BF16)
            waited = (back, both)
            both = shift(both, "fsdp", 2 * (1 + g)).astype(F32)
            total = both if total is None else total + both
            sum_a, sum_b = add(d_a, from_a), add(d_b, from_b)
            sum_o, sum_p = jnp.where(col == 0, sum_a, sum_b), jnp.where(col == 0, sum_b, sum_a)
            own_d.append((sum_o, swap(sum_p, "seq")))
        else:
            keep, give = terms_of(od_own, od_par)
            d_far, = after([d_far], from_a)
            back = shift(d_far, "seq", -2)
            od_par, = after([od_par], from_b, total)
            par_od.append(swap(od_par, "seq"))
            total = total + keep + swap(give, "fsdp").astype(F32)
            z = s // 2
            mine = lax.dynamic_index_in_dim(total, z, 0, keepdims=False)
            total = total.astype(BF16)
            total, = after([total], back)
            pieces = []
            for by in range(1, pairs):
                there = lax.dynamic_index_in_dim(total, (z + by) % pairs, 0, keepdims=False)
                pieces.append(shift(there, "seq", 2 * by))
            near_b = add(d_near_b, back)
            from_p = shift(jnp.where(col == 0, near_b, d_near_a), "seq", -2)
            sum_p = add(jnp.where(col == 0, d_b, d_a), from_p)
            par_od = list(after(par_od, from_p))
            own_d = [(a, *after([b], from_p)) for a, b in own_d]
            for_own = swap(sum_p, "seq")
            for piece in pieces:
                mine = mine + piece.astype(F32)
            n = blocks * shards

            def mirror(i):
                ss, ff = divmod(i, shards)
                return (ss - ss % 2 + ff % 2) * shards + ff - ff % 2 + ss % 2

            crossed = lax.ppermute(mine.astype(BF16), ("seq", "fsdp"), [(i, mirror(i)) for i in range(n)])
            grad_weight = jnp.where(core == col, mine, crossed.astype(F32))
            own = jnp.where(col == 0, d_near_a, near_b)
            own, = after([own], *pieces)
            from_o = shift(own, "seq", -2)
            from_o, = after([from_o], for_own, grad_weight)
            sum_o = add(jnp.where(col == 0, d_a, d_b), from_o)
            own_d.append((sum_o, for_own))

    rel_out = jnp.concatenate([p for g in range(groups) for p in (own_od[g][0], par_od[g][0])], axis=1)
    rel_weight = jnp.concatenate([p for g in range(groups) for p in weight[g]], axis=0)
    image_out = jnp.dot(rel_out, rel_weight, preferred_element_type=F32).astype(BF16)

    def assemble(pieces):
        whole = jnp.zeros((tokens, width * shards), BF16)
        for g in range(groups):
            whole = lax.dynamic_update_slice_in_dim(whole, pieces[g][0], shard[g] * width, 1)
            whole = lax.dynamic_update_slice_in_dim(whole, pieces[g][1], other[g] * width, 1)
        return whole

    grad_q = assemble([(own_od[g][1], par_od[g][1]) for g in range(groups)])
    grad_k = assemble([(own_d[g][0][0], own_d[g][1][0]) for g in range(groups)])
    grad_v = assemble([(own_d[g][0][1], own_d[g][1][1]) for g in range(groups)])
    return image_out[None], grad_q[None], grad_k[None], grad_v[None], grad_weight


def solution(mesh):
    in_specs = (
        P("fsdp", "seq", None),
        P("fsdp", "seq", None),
        P("fsdp", "seq", None),
        P("fsdp", None, None),
        P("fsdp", None, None),
        P("fsdp", None),
        P("fsdp", "seq", None),
    )
    out_specs = (
        P("fsdp", "seq", None),
        P("fsdp", "seq", None),
        P("fsdp", "seq", None),
        P("fsdp", "seq", None),
        P(("fsdp", "seq"), None),
    )
    return jax.shard_map(
        per_device, mesh=mesh, in_specs=in_specs, out_specs=out_specs, check_vma=False
    )
```

```python
import functools
import math

import jax
import jax.numpy as jnp
from jax import lax
from jax.experimental import pallas as pl
from jax.experimental.pallas import tpu as pltpu
from jax.sharding import PartitionSpec as P

HEAD_DIM = 128
STEPS = 4
F32 = jnp.float32
BF16 = jnp.bfloat16


def rows_dot(a, b):
    return lax.dot_general(a, b, (((1,), (1,)), ((), ())), preferred_element_type=F32)


def cols_dot(a, b):
    return lax.dot_general(a, b, (((0,), (0,)), ((), ())), preferred_element_type=F32)


def dot(a, b):
    return jnp.dot(a, b, preferred_element_type=F32)


def attention_body(
    place, q_own, q_par, k_own, v_own, kv_par, near_own, near_par, far, t_k, t_v, g_own, g_par,
    od_own, od_par, d_a, d_b, d_near_a, d_near_b, d_far,
):
    tokens = q_own.shape[0]
    first = place[1] == 0
    scale = 1.0 / math.sqrt(q_own.shape[1])
    to_log2 = scale * math.log2(math.e)

    def by_block(own, par):
        return jnp.where(first, own, par), jnp.where(first, par, own)

    q = by_block(q_own[...], q_par[...])
    g = by_block(g_own[...], g_par[...])
    text = t_k.shape[0] // tokens
    keys = [t_k[i * tokens : (i + 1) * tokens] for i in range(text)]
    keys += [far[0], *by_block(near_own[0], near_par[0]), *by_block(k_own[...], kv_par[0])]
    values = [t_v[i * tokens : (i + 1) * tokens] for i in range(text)]
    values += [far[1], *by_block(near_own[1], near_par[1]), *by_block(v_own[...], kv_par[1])]
    keys_t = [k.T for k in keys]
    values_t = [v.T for v in values]
    sets = [list(range(text)) + list(range(text + i, text + i + STEPS)) for i in range(2)]
    score = [{j: rows_dot(keys[j], q[i]) for j in sets[i]} for i in range(2)]
    prob, low, grad_low = [], [], []
    out_t = []
    for i in range(2):
        peak = functools.reduce(jnp.maximum, [score[i][j] for j in sets[i]])
        peak = jnp.max(peak, axis=0, keepdims=True)
        e = {j: jnp.exp2((score[i][j] - peak) * to_log2) for j in sets[i]}
        total = jnp.sum(functools.reduce(jnp.add, e.values()), axis=0, keepdims=True)
        inverse = 1.0 / total
        prob.append({j: e[j] * inverse for j in sets[i]})
        low.append({j: prob[i][j].astype(BF16) for j in sets[i]})
        out_t.append(functools.reduce(jnp.add, [dot(values_t[j], low[i][j]) for j in sets[i]]))
    outs, dqs = [], []
    for i in range(2):
        out = out_t[i].T.astype(BF16)
        outs.append(out)
        delta = jnp.sum(g[i].T.astype(F32) * out_t[i].astype(BF16).astype(F32), axis=0, keepdims=True)
        grad_low.append({
            j: (prob[i][j] * (rows_dot(values[j], g[i]) - delta)).astype(BF16) for j in sets[i]
        })
        dq = functools.reduce(jnp.add, [dot(keys_t[j], grad_low[i][j]) for j in sets[i]])
        dqs.append((dq * scale).T.astype(BF16))
    for n, (own, par) in enumerate((by_block(*outs), by_block(*dqs))):
        od_own[n] = own
        od_par[n] = par
    for n, ref in enumerate((d_far, d_near_a, d_near_b, d_a, d_b)):
        j = text + n
        users = [i for i in range(2) if j in sets[i]]
        dk = functools.reduce(jnp.add, [dot(grad_low[i][j], q[i]) for i in users])
        dv = functools.reduce(jnp.add, [dot(low[i][j], g[i]) for i in users])
        ref[0] = (dk * scale).astype(BF16)
        ref[1] = dv.astype(BF16)


def attention(place, q, q_par, k, v, kv_par, near_own, near_par, far, t_k, t_v, g_own, g_par):
    tokens = q.shape[0]
    width = q_par.shape[1]
    text = t_k.shape[0]
    heads = width // HEAD_DIM
    whole = lambda rows: pl.BlockSpec((rows, HEAD_DIM), lambda h, place: (0, place[0] * heads + h))
    part = pl.BlockSpec((tokens, HEAD_DIM), lambda h, place: (0, h))
    double = pl.BlockSpec((2, tokens, HEAD_DIM), lambda h, place: (0, 0, h))
    keys = text + STEPS * tokens
    macs = heads * 2 * tokens * HEAD_DIM * (4 * keys + 2 * STEPS * tokens)
    out = jax.ShapeDtypeStruct((2, tokens, width), BF16)
    return pl.pallas_call(
        attention_body,
        out_shape=(out,) * 7,
        grid_spec=pltpu.PrefetchScalarGridSpec(
            num_scalar_prefetch=1,
            grid=(heads,),
            in_specs=[whole(tokens), part, whole(tokens), whole(tokens), double, double, double, double,
                      whole(text), whole(text), part, part],
            out_specs=[double] * 7,
        ),
        compiler_params=pltpu.CompilerParams(vmem_limit_bytes=16 * 1024 * 1024),
        cost_estimate=pl.CostEstimate(
            flops=4 * macs, bytes_accessed=24 * tokens * width * 2, transcendentals=heads * 2 * tokens * keys
        ),
        name="attention",
    )(place, q, q_par, k, v, kv_par, near_own, near_par, far, t_k, t_v, g_own, g_par)


def per_device(image_query, image_key, image_value, text_key, text_value, out_weight, cotangent):
    q, k, v = image_query[0], image_key[0], image_value[0]
    t_k, t_v = text_key[0], text_value[0]
    cot = cotangent[0]
    shards = lax.axis_size("fsdp")
    blocks = lax.axis_size("seq")
    pairs = blocks // 2
    groups = shards // 2
    width = out_weight.shape[0]
    tokens = q.shape[0]
    f, s = lax.axis_index("fsdp"), lax.axis_index("seq")
    col, core, row = s % 2, f % 2, f // 2

    def shift(a, axis, by):
        n = lax.axis_size(axis)
        return lax.ppermute(a, axis, [(i, (i + by) % n) for i in range(n)])

    def swap(a, axis):
        return lax.ppermute(a, axis, [(i, i ^ 1) for i in range(lax.axis_size(axis))])

    shard = [((row + 1 + g) % groups) * 2 + col for g in range(groups)]
    other = [((row + 1 + g) % groups) * 2 + 1 - col for g in range(groups)]

    def after(operands, *others):
        return lax.optimization_barrier((tuple(operands), others))[0]

    every = range(groups)
    last = groups - 1

    def cut(a, index):
        return lax.dynamic_slice_in_dim(a, index * width, width, 1)

    def cut_two(index):
        return jnp.stack([cut(k, index), cut(v, index)])

    half = tokens // 2
    kv_own = [cut_two(shard[g]) for g in every]
    near_own = [shift(kv_own[g], "seq", 2) for g in every]
    kv_par = [swap(cut_two(other[g]), "seq") for g in every]
    held = [shift(out_weight, "fsdp", -2 * (1 + g)) if g < last else out_weight for g in every]
    cot_par, near_par, far, q_par = [], [], [], []
    for g in every:
        kv, = after([kv_par[g]], *near_own[: 1 if g == 0 else groups])
        near_par.append(shift(kv, "seq", 2))
        if g < 2:
            c, = after([cot[g * half : (g + 1) * half]], kv_par[g], near_own[g])
            cot_par.append(swap(c, "seq"))
    for g in every:
        b_near = jnp.where(col == 0, near_par[g], near_own[g])
        far.append(shift(b_near, "seq", 2))
        c, = after([cut(q, other[g])], cot_par[min(g, len(cot_par) - 1)])
        q_par.append(swap(c, "seq"))
    cot_par = jnp.concatenate(cot_par, axis=0)

    weight = []
    for g in every:
        from_core = swap(held[g], "fsdp")
        weight.append((jnp.where(core == col, held[g], from_core), jnp.where(core == col, from_core, held[g])))

    rows = width // blocks

    def terms_of(od_own, od_par):
        terms = cols_dot(od_own[0], cot) + cols_dot(od_par[0], cot_par)
        terms = terms.reshape(pairs, 2, rows, -1)
        keep = lax.dynamic_index_in_dim(terms, core, 1, keepdims=False)
        give = lax.dynamic_index_in_dim(terms, 1 - core, 1, keepdims=False).astype(BF16)
        return keep, give

    def add(a, b):
        return (a.astype(F32) + b.astype(F32)).astype(BF16)

    def run(g, others):
        g_own = rows_dot(cot, weight[g][0]).astype(BF16)
        g_par = rows_dot(cot_par, weight[g][0]).astype(BF16)
        place = jnp.stack([shard[g], col]).astype(jnp.int32)
        g_own, g_par = after([g_own, g_par], *others)
        return attention(
            place, q, q_par[g], k, v, kv_par[g], near_own[g], near_par[g], far[g], t_k, t_v, g_own, g_par
        )

    own_od, par_od, own_d, total = [], [], [], None
    waited = ()
    for g in every:
        od_own, od_par, d_a, d_b, d_near_a, d_near_b, d_far = run(g, waited)
        own_od.append(od_own)
        if g < last:
            back = shift(d_far, "seq", -2)
            od_p, = after([od_par], back)
            par_od.append(swap(od_p, "seq"))
            keep, give = terms_of(od_own, od_par)
            from_a = shift(d_near_a, "seq", -2)
            from_b = shift(add(d_near_b, back), "seq", -2)
            both = (keep + swap(give, "fsdp").astype(F32)).astype(BF16)
            waited = (back, both)
            both = shift(both, "fsdp", 2 * (1 + g)).astype(F32)
            total = both if total is None else total + both
            sum_a, sum_b = add(d_a, from_a), add(d_b, from_b)
            sum_o, sum_p = jnp.where(col == 0, sum_a, sum_b), jnp.where(col == 0, sum_b, sum_a)
            own_d.append((sum_o, swap(sum_p, "seq")))
        else:
            keep, give = terms_of(od_own, od_par)
            d_far, = after([d_far])
            back = shift(d_far, "seq", -2)
            od_par, = after([od_par], from_b, total)
            par_od.append(swap(od_par, "seq"))
            total = total + keep + swap(give, "fsdp").astype(F32)
            z = s // 2
            mine = lax.dynamic_index_in_dim(total, z, 0, keepdims=False)
            total = total.astype(BF16)
            total, = after([total], back)
            pieces = []
            for by in range(1, pairs):
                there = lax.dynamic_index_in_dim(total, (z + by) % pairs, 0, keepdims=False)
                pieces.append(shift(there, "seq", 2 * by))
            near_b = add(d_near_b, back)
            from_p = shift(jnp.where(col == 0, near_b, d_near_a), "seq", -2)
            sum_p = add(jnp.where(col == 0, d_b, d_a), from_p)
            par_od = list(after(par_od, from_p))
            own_d = [(a, *after([b], from_p)) for a, b in own_d]
            for_own = swap(sum_p, "seq")
            for piece in pieces:
                mine = mine + piece.astype(F32)
            n = blocks * shards

            def mirror(i):
                ss, ff = divmod(i, shards)
                return (ss - ss % 2 + ff % 2) * shards + ff - ff % 2 + ss % 2

            crossed = lax.ppermute(mine.astype(BF16), ("seq", "fsdp"), [(i, mirror(i)) for i in range(n)])
            grad_weight = jnp.where(core == col, mine, crossed.astype(F32))
            own = jnp.where(col == 0, d_near_a, near_b)
            own, = after([own], *pieces)
            from_o = shift(own, "seq", -2)
            from_o, = after([from_o], for_own)
            sum_o = add(jnp.where(col == 0, d_a, d_b), from_o)
            own_d.append((sum_o, for_own))

    rel_out = jnp.concatenate([p for g in range(groups) for p in (own_od[g][0], par_od[g][0])], axis=1)
    rel_weight = jnp.concatenate([p for g in range(groups) for p in weight[g]], axis=0)
    image_out = jnp.dot(rel_out, rel_weight, preferred_element_type=F32).astype(BF16)

    def assemble(pieces):
        whole = jnp.zeros((tokens, width * shards), BF16)
        for g in range(groups):
            whole = lax.dynamic_update_slice_in_dim(whole, pieces[g][0], shard[g] * width, 1)
            whole = lax.dynamic_update_slice_in_dim(whole, pieces[g][1], other[g] * width, 1)
        return whole

    grad_q = assemble([(own_od[g][1], par_od[g][1]) for g in range(groups)])
    grad_k = assemble([(own_d[g][0][0], own_d[g][1][0]) for g in range(groups)])
    grad_v = assemble([(own_d[g][0][1], own_d[g][1][1]) for g in range(groups)])
    return image_out[None], grad_q[None], grad_k[None], grad_v[None], grad_weight


def solution(mesh):
    in_specs = (
        P("fsdp", "seq", None),
        P("fsdp", "seq", None),
        P("fsdp", "seq", None),
        P("fsdp", None, None),
        P("fsdp", None, None),
        P("fsdp", None),
        P("fsdp", "seq", None),
    )
    out_specs = (
        P("fsdp", "seq", None),
        P("fsdp", "seq", None),
        P("fsdp", "seq", None),
        P("fsdp", "seq", None),
        P(("fsdp", "seq"), None),
    )
    return jax.shard_map(
        per_device, mesh=mesh, in_specs=in_specs, out_specs=out_specs, check_vma=False
    )
```
